32 devices in a mesh: chan: 2 (over x), tm: 8 (over z, y), dp: 2 (over core).
Axes of the slice: x: 2, y: 2, z: 4, core: 2. Of those that a mesh axis runs over, the one named last changes fastest.
Arguments:
- contexts: bfloat16 [512, 4, 16384], P('tm', 'dp', 'chan'), may hold values from -6 to 6
- cotangent: bfloat16 [512, 4, 16384], P('tm', 'dp', 'chan'), may hold values from -6 to 6
- w_in: bfloat16 [16384, 8192], P('chan', 'tm'), may hold values from -0.046875 to 0.046875
- w_out: bfloat16 [8192, 16384], P('tm', 'chan'), may hold values from -0.0625 to 0.0625
- time_weight: bfloat16 [512, 512], replicated, may hold values from -0.25 to 0.25
Outputs:
- grad_contexts: bfloat16 [512, 4, 16384], P('tm', 'dp', 'chan')
- grad_w_in: float32 [16384, 8192], P('chan', ('tm', 'dp'))
- grad_w_out: float32 [8192, 16384], P(('tm', 'dp'), 'chan')
- grad_time: float32 [512, 512], replicated
The draws below stay inside these ranges and needn't reach their ends.
All inputs are finite; a program needn't handle non-finite values.
Results may differ from the reference program's by a relative error of at most 0.0057.
Values may be sent and summed in bfloat16 or wider, within the bound.
A program may use at most 384 MiB of HBM per device.

```python
import math
import jax
import jax.numpy as jnp

CHANNELS = 16384
HIDDEN_SIZE = 8192
LEN = 512
WIN = 4


def block_levels(rng, extent, cuts, least, top_value):
    def one(axis_at, blocks):
        draws = jax.random.uniform(jax.random.fold_in(jax.random.fold_in(rng, 6), axis_at), (blocks,), jnp.float32, least / len(cuts), top_value / len(cuts))
        return jnp.repeat(jnp.exp(draws), extent[axis_at] // blocks).reshape((-1,) + (1,) * (len(extent) - axis_at - 1))

    loudness = one(*cuts[0])
    for cut in cuts[1:]:
        loudness = loudness * one(*cut)
    return loudness


def gaussian(key, extent, scale, bound, pieces=(), held_as=jnp.bfloat16):
    gain = block_levels(key, extent, pieces, -0.22, 0.18) if pieces else 1.0
    array = jax.random.normal(key, extent, jnp.float32) * scale * gain
    return jnp.minimum(jnp.maximum(array, -bound), bound).astype(held_as)


def setup_inputs(seed: int = 0) -> dict:
    splits = jax.random.split(jax.random.key(seed), 6)
    contexts = gaussian(splits[0], (LEN, WIN, CHANNELS), 1.0, 6.0, ((0, 8), (1, 2), (2, 2)))
    cotangent = gaussian(splits[1], (LEN, WIN, CHANNELS), 1.0, 6.0, ((0, 8), (1, 2), (2, 2)))
    w_in = gaussian(splits[2], (CHANNELS, HIDDEN_SIZE), CHANNELS ** -0.5, 0.046875, ((0, 2), (1, 8)))
    w_out = gaussian(splits[3], (HIDDEN_SIZE, CHANNELS), HIDDEN_SIZE ** -0.5, 0.0625, ((0, 8), (1, 2)))
    time_weight = gaussian(splits[4], (LEN, LEN), LEN ** -0.5, 0.25)
    return dict(contexts=contexts, cotangent=cotangent, w_in=w_in, w_out=w_out, time_weight=time_weight)


tanh_scale = math.sqrt(2.0 / math.pi)
cubic_term = 0.044715

def gelu_pair(value):
    inner = jnp.tanh(tanh_scale * (value + cubic_term * value * value * value))
    result = 0.5 * value * (1.0 + inner)
    slope = 0.5 * (1.0 + inner) + 0.5 * value * (1.0 - inner * inner) * tanh_scale * (1.0 + 3.0 * cubic_term * value * value)
    return (result, slope)

def reference(contexts, cotangent, w_in, w_out, time_weight):
    length, windows, channels = contexts.shape
    flat_x = contexts.reshape(length, windows * channels)
    pre_time = jnp.dot(time_weight, flat_x, preferred_element_type=jnp.float32)
    act_time, slope_time = gelu_pair(pre_time)
    mixed = (flat_x.astype(jnp.float32) + act_time).astype(jnp.bfloat16).reshape(length * windows, channels)
    grad_rows = cotangent.reshape(length * windows, channels)
    hidden_pre = jnp.dot(mixed, w_in, preferred_element_type=jnp.float32)
    hidden_grad = jnp.dot(grad_rows, w_out.T, preferred_element_type=jnp.float32)
    act_hidden, slope_hidden = gelu_pair(hidden_pre)
    activation = act_hidden.astype(jnp.bfloat16)
    pre_grad = (hidden_grad * slope_hidden).astype(jnp.bfloat16)
    grad_w_in = jnp.dot(mixed.T, pre_grad, preferred_element_type=jnp.float32)
    grad_w_out = jnp.dot(activation.T, grad_rows, preferred_element_type=jnp.float32)
    mixed_grad = grad_rows.astype(jnp.float32) + jnp.dot(pre_grad, w_in.T, preferred_element_type=jnp.float32)
    time_gate = (mixed_grad.reshape(length, windows * channels) * slope_time).astype(jnp.bfloat16)
    back = jnp.dot(time_weight.T, time_gate, preferred_element_type=jnp.float32)
    grad_contexts = (mixed_grad.reshape(length, windows * channels) + back).astype(jnp.bfloat16).reshape(length, windows, channels)
    grad_time = jnp.dot(time_gate, flat_x.T, preferred_element_type=jnp.float32)
    return (grad_contexts, grad_w_in, grad_w_out, grad_time)
```

```python
import math

import jax
import jax.numpy as jnp
from jax import lax
from jax.sharding import PartitionSpec as P

tanh_scale = math.sqrt(2.0 / math.pi)
cubic_term = 0.044715


def gelu_pair(value):
    inner = jnp.tanh(tanh_scale * (value + cubic_term * value * value * value))
    result = 0.5 * value * (1.0 + inner)
    slope = 0.5 * (1.0 + inner) + 0.5 * value * (1.0 - inner * inner) * tanh_scale * (
        1.0 + 3.0 * cubic_term * value * value
    )
    return (result, slope)


def hidden_finish(hidden_pre, hidden_grad):
    act_hidden, slope_hidden = gelu_pair(hidden_pre)
    return (act_hidden.astype(jnp.bfloat16), (hidden_grad * slope_hidden).astype(jnp.bfloat16))


def dot(lhs, rhs, lhs_dim, rhs_dim):
    return lax.dot_general(
        lhs, rhs, (((lhs_dim,), (rhs_dim,)), ((), ())), preferred_element_type=jnp.float32
    )


def shifted(value, axis, count, step):
    return lax.ppermute(value, axis, [(i, (i + step) % count) for i in range(count)])


def body(chan_count, tm_count, dp_count):
    def chan_sum(part):
        total = part
        narrow = part.astype(jnp.bfloat16)
        for step in range(1, chan_count):
            total = total + shifted(narrow, "chan", chan_count, step).astype(jnp.float32)
        return total

    def dp_scatter(product, split):
        here = lax.axis_index("dp")
        arrived = []
        for step in range(1, dp_count):
            there = (here + step) % dp_count
            term = product(lax.dynamic_slice_in_dim(split, there * (split.shape[1] // dp_count), split.shape[1] // dp_count, 1))
            arrived.append(shifted(term.astype(jnp.bfloat16), "dp", dp_count, step))
        size = split.shape[1] // dp_count
        total = product(lax.dynamic_slice_in_dim(split, here * size, size, 1))
        for term in arrived:
            total = total + term.astype(jnp.float32)
        return total

    def on_device(contexts, cotangent, w_in, w_out, time_weight):
        local_len, windows, width = contexts.shape
        own_width = width // tm_count
        position = lax.axis_index("tm")

        def own(array):
            return lax.dynamic_slice_in_dim(array, position * own_width, own_width, 1)

        xs, dys, mixeds, acts, grads, feats = [], [], [], [], [], []
        for b in range(windows):
            x = lax.all_gather(contexts[:, b, :], "tm", axis=0, tiled=True)
            dy = lax.all_gather(cotangent[:, b, :], "tm", axis=0, tiled=True)
            xs.append(x)
            dys.append(dy)
        for b in range(windows):
            x, dy = xs[b], dys[b]
            act_time, _ = gelu_pair(dot(time_weight, x, 1, 0))
            mixed = (x.astype(jnp.float32) + act_time).astype(jnp.bfloat16)
            hidden_pre = chan_sum(dot(mixed, w_in, 1, 0))
            hidden_grad = chan_sum(dot(dy, w_out, 1, 1))
            activation, pre_grad = hidden_finish(hidden_pre, hidden_grad)
            mixeds.append(mixed)
            acts.append(activation)
            grads.append(pre_grad)
            feature = dot(pre_grad, w_in, 1, 1).astype(jnp.bfloat16)
            feats.append(lax.psum_scatter(feature, "tm", scatter_dimension=1, tiled=True))

        outs = []
        time_part = None
        for b in range(windows):
            x_own, dy_own = own(xs[b]), own(dys[b])
            _, slope = gelu_pair(dot(time_weight, x_own, 1, 0))
            mixed_grad = dy_own.astype(jnp.float32) + feats[b].astype(jnp.float32)
            gate = (mixed_grad * slope).astype(jnp.bfloat16)
            back = dot(time_weight, gate, 0, 0)
            outs.append(
                lax.all_to_all(
                    (mixed_grad + back).astype(jnp.bfloat16), "tm", 0, 1, tiled=True
                )
            )
            term = dot(gate, x_own, 1, 1)
            time_part = term if time_part is None else time_part + term
        grad_time = lax.psum(time_part, ("chan", "tm", "dp"))
        grad_contexts = jnp.stack(outs, axis=1)

        mixed_rows = jnp.concatenate(mixeds, axis=0)
        dy_rows = jnp.concatenate(dys, axis=0)
        grad_w_in = dp_scatter(
            lambda part: dot(mixed_rows, part, 0, 0), jnp.concatenate(grads, axis=0)
        )
        grad_w_out = dp_scatter(
            lambda part: dot(part, dy_rows, 0, 0), jnp.concatenate(acts, axis=0)
        )
        return (grad_contexts, grad_w_in, grad_w_out, grad_time)

    return on_device


def solution(mesh):
    return jax.shard_map(
        body(mesh.shape["chan"], mesh.shape["tm"], mesh.shape["dp"]),
        mesh=mesh,
        in_specs=(
            P("tm", "dp", "chan"),
            P("tm", "dp", "chan"),
            P("chan", "tm"),
            P("tm", "chan"),
            P(),
        ),
        out_specs=(P("tm", "dp", "chan"), P("chan", ("tm", "dp")), P(("tm", "dp"), "chan"), P()),
        check_vma=False,
    )
```

```python
import math

import jax
import jax.numpy as jnp
from jax import lax
from jax.sharding import PartitionSpec as P

tanh_scale = math.sqrt(2.0 / math.pi)
cubic_term = 0.044715


def gelu_pair(value):
    inner = jnp.tanh(tanh_scale * (value + cubic_term * value * value * value))
    result = 0.5 * value * (1.0 + inner)
    slope = 0.5 * (1.0 + inner) + 0.5 * value * (1.0 - inner * inner) * tanh_scale * (
        1.0 + 3.0 * cubic_term * value * value
    )
    return (result, slope)


def hidden_finish(hidden_pre, hidden_grad):
    act_hidden, slope_hidden = gelu_pair(hidden_pre)
    return (act_hidden.astype(jnp.bfloat16), (hidden_grad * slope_hidden).astype(jnp.bfloat16))


def dot(lhs, rhs, lhs_dim, rhs_dim):
    return lax.dot_general(
        lhs, rhs, (((lhs_dim,), (rhs_dim,)), ((), ())), preferred_element_type=jnp.float32
    )


def shifted(value, axis, count, step):
    return lax.ppermute(value, axis, [(i, (i + step) % count) for i in range(count)])


def body(chan_count, tm_count, dp_count):
    def chan_sum(part):
        total = part
        narrow = part.astype(jnp.bfloat16)
        for step in range(1, chan_count):
            total = total + shifted(narrow, "chan", chan_count, step).astype(jnp.float32)
        return total

    def dp_scatter(product, split):
        here = lax.axis_index("dp")
        arrived = []
        for step in range(1, dp_count):
            there = (here + step) % dp_count
            term = product(lax.dynamic_slice_in_dim(split, there * (split.shape[1] // dp_count), split.shape[1] // dp_count, 1))
            arrived.append(shifted(term.astype(jnp.bfloat16), "dp", dp_count, step))
        size = split.shape[1] // dp_count
        total = product(lax.dynamic_slice_in_dim(split, here * size, size, 1))
        for term in arrived:
            total = total + term.astype(jnp.float32)
        return total

    outer = min(4, tm_count)
    inner = tm_count // outer

    def line_gather(block):
        rows = block.shape[0]
        position = lax.axis_index("tm")
        far, near = position // inner, position % inner
        up = [(i, i + inner) for i in range(tm_count - inner)]
        down = [(i + inner, i) for i in range(tm_count - inner)]
        lower, upper = [block], [block]
        for _ in range(1, outer):
            lower.append(lax.ppermute(lower[-1], "tm", up))
            upper.append(lax.ppermute(upper[-1], "tm", down))
        whole = jnp.zeros((rows * tm_count, block.shape[1]), block.dtype)
        for k in range(outer):
            piece = block if k == 0 else jnp.where(far + k < outer, upper[k], lower[outer - k])
            line = (far + k) % outer
            for step in range(inner):
                if step == 0:
                    landed = piece
                else:
                    pairs = [
                        (i, i // inner * inner + (i % inner + step) % inner)
                        for i in range(tm_count)
                    ]
                    landed = lax.ppermute(piece, "tm", pairs)
                owner = line * inner + (near + inner - step) % inner
                whole = lax.dynamic_update_slice(whole, landed, (owner * rows, 0))
        return whole

    def full_sum(part):
        rows = part.shape[0] // tm_count
        terms = lax.all_to_all(part, "tm", 0, 0, tiled=True)
        total = terms.reshape(tm_count, rows, part.shape[1]).sum(axis=0)
        for axis, count in (("chan", chan_count), ("dp", dp_count)):
            if count == 2:
                total = total + shifted(total, axis, count, 1)
            else:
                total = lax.psum(total, axis)
        return lax.all_to_all(jnp.tile(total, (tm_count, 1)), "tm", 0, 0, tiled=True)

    def on_device(contexts, cotangent, w_in, w_out, time_weight):
        local_len, windows, width = contexts.shape
        own_width = width // tm_count
        position = lax.axis_index("tm")

        def own(array):
            return lax.dynamic_slice_in_dim(array, position * own_width, own_width, 1)

        xs, dys, mixeds, acts, grads, feats = [], [], [], [], [], []
        for b in range(windows):
            dy = lax.all_gather(cotangent[:, b, :], "tm", axis=0, tiled=True)
            block = contexts[:, b, :]
            if b > 0:
                block, xs[-1] = lax.optimization_barrier((block, xs[-1]))
            x = line_gather(block)
            xs.append(x)
            dys.append(dy)
        for b in range(windows):
            if b > 0:
                xs[b], dys[b], grads[-1] = lax.optimization_barrier((xs[b], dys[b], grads[-1]))
            x, dy = xs[b], dys[b]
            act_time, _ = gelu_pair(dot(time_weight, x, 1, 0))
            mixed = (x.astype(jnp.float32) + act_time).astype(jnp.bfloat16)
            hidden_pre = chan_sum(dot(mixed, w_in, 1, 0))
            hidden_grad = chan_sum(dot(dy, w_out, 1, 1))
            activation, pre_grad = hidden_finish(hidden_pre, hidden_grad)
            mixeds.append(mixed)
            acts.append(activation)
            grads.append(pre_grad)
            feature = dot(pre_grad, w_in, 1, 1).astype(jnp.bfloat16)
            feats.append(lax.psum_scatter(feature, "tm", scatter_dimension=1, tiled=True))

        outs = []
        time_part = None
        for b in range(windows):
            x_own, dy_own = own(xs[b]), own(dys[b])
            _, slope = gelu_pair(dot(time_weight, x_own, 1, 0))
            mixed_grad = dy_own.astype(jnp.float32) + feats[b].astype(jnp.float32)
            gate = (mixed_grad * slope).astype(jnp.bfloat16)
            back = dot(time_weight, gate, 0, 0)
            outs.append(
                lax.all_to_all(
                    (mixed_grad + back).astype(jnp.bfloat16), "tm", 0, 1, tiled=True
                )
            )
            term = dot(gate, x_own, 1, 1)
            time_part = term if time_part is None else time_part + term
        grad_time = full_sum(time_part)
        grad_contexts = jnp.stack(outs, axis=1)

        mixed_rows = jnp.concatenate(mixeds, axis=0)
        dy_rows = jnp.concatenate(dys, axis=0)
        grad_w_in = dp_scatter(
            lambda part: dot(mixed_rows, part, 0, 0), jnp.concatenate(grads, axis=0)
        )
        grad_w_out = dp_scatter(
            lambda part: dot(part, dy_rows, 0, 0), jnp.concatenate(acts, axis=0)
        )
        return (grad_contexts, grad_w_in, grad_w_out, grad_time)

    return on_device


def solution(mesh):
    return jax.shard_map(
        body(mesh.shape["chan"], mesh.shape["tm"], mesh.shape["dp"]),
        mesh=mesh,
        in_specs=(
            P("tm", "dp", "chan"),
            P("tm", "dp", "chan"),
            P("chan", "tm"),
            P("tm", "chan"),
            P(),
        ),
        out_specs=(P("tm", "dp", "chan"), P("chan", ("tm", "dp")), P(("tm", "dp"), "chan"), P()),
        check_vma=False,
    )
```
